768 devices in a mesh: grp: 16 (over y, core), rank: 48 (over z, x).
Axes of the slice: x: 4, y: 8, z: 12, core: 2. Of those that a mesh axis runs over, the one named last changes fastest.
Arguments:
- a_blocks: bfloat16 [6144, 8, 128, 128], P(('grp', 'rank')), may hold values from -0.5 to 0.5
- a_cols: int32 [6144, 8], P(('grp', 'rank')), may hold values from 0 to 6143, as said below
- p_blocks: bfloat16 [6144, 128, 128], P(('grp', 'rank')), may hold values from -1.796875 to 1.796875
- agg_grp: int32 [6144], P(('grp', 'rank')), may hold values from 0 to 15
- c_slot: int32 [6144, 8], P(('grp', 'rank')), may hold values from 0 to 1
Outputs:
- coarse: bfloat16 [768, 2, 128, 128], P(('grp', 'rank'))
The draws below stay inside these ranges and needn't reach their ends.
Inputs may be any that keep to these rules, and one draw needn't show every extreme that they name: a_cols[n, 0] = n. Every column lies in the group of its row: a_cols[n, k] // (8 * 48) = n // (8 * 48). For each device and each other device of its group, all columns of the first device's rows that lie on the second device name one and the same row of it.
All inputs are finite; a program needn't handle non-finite values.
Results may differ from the reference program's by a relative error of at most 0.0049.
Values may be sent and summed in bfloat16 or wider, within the bound.
A program may use at most 64 MiB of HBM per device.

```python
import math
import jax
import jax.numpy as jnp
import numpy as np
from jax import lax

BLOCK = 128
NNZ = 8
ROWS = 8
SLOTS = 2
FINE = 6144
COARSE = 768
N_GRP = 16
N_RANK = 48


def draw_a_cols(key, part):
    key = jax.random.fold_in(key, 11)
    key_couple, key_peer = jax.random.split(key)
    devices = N_GRP * N_RANK
    device = jnp.arange(FINE, dtype=jnp.int32) // ROWS
    group = device // N_RANK
    couple = jax.random.randint(key_couple, (devices, N_RANK), 0, ROWS, dtype=jnp.int32)
    peers = jax.random.randint(key_peer, (FINE, NNZ - 1), 0, N_RANK, dtype=jnp.int32)
    column_device = group[:, None] * N_RANK + peers
    within = couple[device[:, None], peers]
    others = column_device * ROWS + within
    diagonal = jnp.arange(FINE, dtype=jnp.int32)[:, None]
    return jnp.concatenate([diagonal, others], axis=1).astype(jnp.int32)


def plant(array, rng, low, top_value):
    place = [jax.random.randint(jax.random.fold_in(rng, axis), (), 0, length) for axis, length in enumerate(array.shape)]
    longest = array.shape.index(max(array.shape))
    neighbour = place[:longest] + [(place[longest] + 1) % array.shape[longest]] + place[longest + 1:]
    return array.at[tuple(place)].set(low).at[tuple(neighbour)].set(top_value)


def block_levels(own_key, extent, shards, low, high):
    level = 1.0
    for axis_at, shards_of in shards:
        draws = jax.random.uniform(jax.random.fold_in(jax.random.fold_in(own_key, 6), axis_at), (shards_of,), jnp.float32, low / len(shards), high / len(shards))
        level = level * jnp.repeat(jnp.exp(draws), extent[axis_at] // shards_of).reshape((-1,) + (1,) * (len(extent) - 1 - axis_at))
    return level


def rank_table(count, lean):
    weights = [(1 << 20) // math.isqrt(rank ** lean) + 1 for rank in range(1, count + 1)]
    width = 1 + sum(weights) // (1 << 30)
    return np.cumsum(np.array([max(1, weight // width) for weight in weights]))


def ranked(key, shape, count, skew):
    grid = rank_table(count, skew)
    ticket = jax.random.randint(jax.random.fold_in(key, 1), shape, 0, int(grid[count - 1]))
    standing = jnp.searchsorted(jnp.asarray(grid, jnp.int32), ticket, side="right")
    return jax.random.permutation(jax.random.fold_in(key, 2), count)[standing].astype(jnp.int32)


def bell_draw(stream_key, dims, deviation, bound, cuts=(), kind=jnp.bfloat16):
    entries = deviation * jax.random.normal(stream_key, dims, jnp.float32)
    if cuts:
        entries = entries * block_levels(stream_key, dims, cuts, -0.22, 0.18)
    return jnp.clip(entries, -bound, bound).astype(kind)


def setup_inputs(seed: int = 0) -> dict:
    seeds = jax.random.split(jax.random.key(seed), 6)
    return {
        "a_blocks": bell_draw(seeds[0], (FINE, NNZ, BLOCK, BLOCK), BLOCK ** -0.5, 0.5, ((0, 768),)),
        "a_cols": draw_a_cols(jax.random.fold_in(seeds[5], 71), 0),
        "p_blocks": bell_draw(seeds[2], (FINE, BLOCK, BLOCK), 0.3, 1.796875, ((0, 768),)),
        "agg_grp": plant(ranked(seeds[3], (FINE,), N_GRP, 2), jax.random.fold_in(seeds[3], 3), 0, N_GRP - 1).astype(jnp.int32),
        "c_slot": plant(jax.random.randint(seeds[4], (FINE, NNZ), 0, SLOTS), jax.random.fold_in(seeds[4], 1), 0, SLOTS - 1).astype(jnp.int32),
    }


def reference(a_blocks, a_cols, p_blocks, agg_grp, c_slot):
    owner_rank = (jnp.arange(FINE, dtype=jnp.int32) // ROWS) % N_RANK
    target = (agg_grp * N_RANK + owner_rank) * SLOTS
    start_acc = jnp.zeros((COARSE * SLOTS, BLOCK, BLOCK), jnp.float32)

    def step(acc, device):
        start = (device * ROWS).astype(jnp.int32)
        a_rows = lax.dynamic_slice_in_dim(a_blocks, start, ROWS, 0).astype(jnp.float32)
        cols = lax.dynamic_slice_in_dim(a_cols, start, ROWS, 0)
        p_rows = lax.dynamic_slice_in_dim(p_blocks, start, ROWS, 0).astype(jnp.float32)
        chosen = jnp.take(p_blocks, cols, axis=0).astype(jnp.float32)
        product = jnp.einsum("qkxy,qkyz->qkxz", a_rows, chosen, precision=lax.Precision.HIGHEST)
        product = lax.optimization_barrier(product.astype(jnp.bfloat16)).astype(jnp.float32)
        term = jnp.einsum("qyx,qkyz->qkxz", p_rows, product, precision=lax.Precision.HIGHEST)
        rows_target = lax.dynamic_slice_in_dim(target, start, ROWS, 0)
        rows_slot = lax.dynamic_slice_in_dim(c_slot, start, ROWS, 0)
        index = (rows_target[:, None] + rows_slot).reshape(-1)
        acc = acc.at[index].add(term.reshape(-1, BLOCK, BLOCK))
        return acc, None

    acc, _ = lax.scan(step, start_acc, jnp.arange(FINE // ROWS, dtype=jnp.int32))
    return acc.reshape(COARSE, SLOTS, BLOCK, BLOCK).astype(jnp.bfloat16)
```

```python
import functools

import jax
import jax.numpy as jnp
from jax import lax
from jax.experimental import pallas as pl
from jax.experimental.pallas import tpu as pltpu
from jax.sharding import PartitionSpec as P

SLOTS = 2
CORES = 2
X = 4
Z = 12
CHUNKS = 4
STAGGER = 2

MESH = pl.DeviceIdType.MESH
NT = (((1,), (1,)), ((), ()))


def kernel(
    sizes,
    cols,
    agg,
    slot,
    p_ref,
    a_hbm,
    out_ref,
    a_ref,
    ring,
    stage,
    table,
    sums,
    outgoing,
    incoming,
    total,
    table_smem,
    place,
    a_sem,
    table_sem,
    table_send,
    table_recv,
    ring_send,
    ring_recv,
    x_send,
    x_recv,
    sum_send,
    sum_recv,
    *chosen,
):
    xs, zs, groups, rows, width, order, chunks, stagger = sizes
    ys = groups // CORES
    half = zs // 2
    part = order // chunks
    ranks = xs * zs
    grp = lax.axis_index("grp")
    rank = lax.axis_index("rank")
    z, x = lax.div(rank, xs), lax.rem(rank, xs)
    y, core = lax.div(grp, CORES), lax.rem(grp, CORES)

    def rank_at(dx, dz):
        return {"rank": lax.rem(z + dz + zs, zs) * xs + lax.rem(x + dx, xs)}

    def grp_at(hop):
        dy, dc = hop // CORES, hop % CORES
        return lax.rem(y + dy, ys) * CORES + lax.rem(core + dc, CORES)

    neighbours = [rank_at(0, 1), rank_at(0, -1)]
    neighbours += [rank_at(d, 0) for d in range(1, xs)]
    neighbours += [{"grp": grp_at(hop)} for hop in range(1, groups)]
    barrier = pltpu.get_barrier_semaphore()
    for device in neighbours:
        pl.semaphore_signal(barrier, inc=1, device_id=device, device_id_type=MESH)
    a_copy = pltpu.make_async_copy(a_hbm, a_ref, a_sem)
    a_copy.start()

    for w in range(rows):
        turned = p_ref[w].astype(jnp.float32).T.astype(jnp.bfloat16)
        for c in range(chunks):
            ring[c, 0, w] = turned[c * part : (c + 1) * part]

    lane = lax.broadcasted_iota(jnp.int32, (8, 128), 1)
    base = grp * (ranks * rows)

    def want(e, held):
        local = cols[lax.div(e, width), lax.rem(e, width)] - base
        peer, within = lax.div(local, rows), lax.rem(local, rows)
        rx = lax.rem(lax.rem(peer, xs) - x + xs, xs)
        j = lax.rem(z - lax.div(peer, xs) + zs, zs)
        spot = jnp.where(j < half, 2 * j - 1, 2 * (zs - j))
        spot = jnp.where(j == 0, 0, jnp.where(j == half, zs - 1, spot))
        place[e] = jnp.where(peer == rank, ranks + within, rx * zs + spot)
        return jnp.maximum(held, jnp.where(lane == peer, within, 0))

    table[0] = lax.fori_loop(0, rows * width, want, jnp.zeros((8, 128), jnp.int32))

    pl.semaphore_wait(barrier, len(neighbours))

    def table_copy(d):
        return pltpu.make_async_remote_copy(
            src_ref=table.at[0],
            dst_ref=table.at[xs - d],
            send_sem=table_send.at[d - 1],
            recv_sem=table_recv.at[xs - d - 1],
            device_id=rank_at(d, 0),
            device_id_type=MESH,
        )

    def ring_copy(c, s, down):
        if down:
            src, dst = (zs - s + 1) % zs, zs - s
        else:
            src, dst = s - 1, s
        source, target = ring.at[c, src], ring.at[c, dst]
        if s == half:
            which = pl.ds(down * (rows // 2), rows // 2)
            source, target = source.at[which], target.at[which]
        return pltpu.make_async_remote_copy(
            src_ref=source,
            dst_ref=target,
            send_sem=ring_send.at[c, s - 1, down],
            recv_sem=ring_recv.at[c, s - 1, down],
            device_id=rank_at(0, -1 if down else 1),
            device_id_type=MESH,
        )

    def x_copy(c, d, start, count):
        return pltpu.make_async_remote_copy(
            src_ref=stage.at[c, d - 1, pl.ds(start, count)],
            dst_ref=chosen[c].at[pl.ds((xs - d) * zs + start, count)],
            send_sem=x_send.at[c, d - 1],
            recv_sem=x_recv.at[c, xs - d - 1],
            device_id=rank_at(d, 0),
            device_id_type=MESH,
        )

    def sum_copy(c, hop):
        return pltpu.make_async_remote_copy(
            src_ref=outgoing.at[c, hop - 1],
            dst_ref=incoming.at[c, hop - 1],
            send_sem=sum_send.at[c],
            recv_sem=sum_recv.at[c],
            device_id={"grp": grp_at(hop)},
            device_id_type=MESH,
        )

    def pick(blocks, index):
        held = blocks[0]
        for w in range(1, rows):
            held = jnp.where(index == w, blocks[w], held)
        return held

    def step(c, s):
        if s > 0:
            ring_copy(c, s, 0).wait_recv()
            ring_copy(c, s, 1).wait_recv()
        if s < half:
            ring_copy(c, s + 1, 0).start()
            ring_copy(c, s + 1, 1).start()
        if c == 0 and s == 0:
            for d in range(1, xs):
                table_copy(d).wait_recv()
            fetch = pltpu.make_async_copy(table, table_smem, table_sem)
            fetch.start()
            fetch.wait()
        if s == 0 or s == half:
            hops = [s]
        else:
            hops = [s, zs - s]
        start = 0 if s == 0 else 2 * s - 1
        for at, j in enumerate(hops):
            blocks = [ring[c, j, w] for w in range(rows)]
            spot = start + at
            source = lax.rem(z - j + zs, zs) * xs + x
            if j == 0:
                for w in range(rows):
                    chosen[c][ranks + w] = blocks[w]
                chosen[c][0] = blocks[0]
            else:
                chosen[c][spot] = pick(blocks, table_smem[0, 0, source])
            for d in range(1, xs):
                stage[c, d - 1, spot] = pick(blocks, table_smem[d, 0, source])
        for d in range(1, xs):
            x_copy(c, d, start, len(hops)).start()

    def compute(c):
        for d in range(1, xs):
            x_copy(c, d, 0, zs).wait_recv()

        def row(n, carry):
            products = []
            for k in range(width):
                q = chosen[c][place[n * width + k]]
                product = lax.dot_general(
                    q, a_ref[n * width + k], NT, preferred_element_type=jnp.float32
                )
                products.append(product.astype(jnp.bfloat16))
            term = jnp.dot(
                jnp.concatenate(products, axis=0),
                p_ref[n],
                preferred_element_type=jnp.float32,
            )
            for s in range(SLOTS):
                held = jnp.zeros((part, order), jnp.float32)
                for k in range(width):
                    mine = term[k * part : (k + 1) * part]
                    held = held + jnp.where(slot[n, k] == s, mine, 0.0)
                sums[n, s] = held
            return carry

        lax.fori_loop(0, rows, row, 0)
        mine = pl.ds(c * part, part)
        for hop in range(groups):
            target = grp_at(hop)
            for s in range(SLOTS):
                held = jnp.zeros((part, order), jnp.float32)
                for n in range(rows):
                    held = held + jnp.where(agg[n] == target, sums[n, s], 0.0)
                if hop == 0:
                    total[s, mine] = held
                else:
                    outgoing[c, hop - 1, s] = held.astype(jnp.bfloat16)
            if hop > 0:
                sum_copy(c, hop).start()

    def whole_sum(c):
        return pltpu.make_async_remote_copy(
            src_ref=outgoing.at[c],
            dst_ref=incoming.at[c],
            send_sem=sum_send.at[c],
            recv_sem=sum_recv.at[c],
            device_id={"grp": grp_at(1)},
            device_id_type=MESH,
        )

    def finish(c):
        whole_sum(c).wait_recv()
        mine = pl.ds(c * part, part)
        for s in range(SLOTS):
            held = total[s, mine]
            for hop in range(1, groups):
                held = held + incoming[c, hop - 1, s].astype(jnp.float32)
            total[s, mine] = held

    for d in range(1, xs):
        table_copy(d).start()

    work = []
    for c in range(chunks):
        for s in range(half + 1):
            work.append((s + stagger * c, c, functools.partial(step, c, s)))
        work.append((half + stagger * c + 0.5, c, functools.partial(compute, c)))
    for _, c, task in sorted(work, key=lambda w: w[:2]):
        if task.func is compute and c == 0:
            a_copy.wait()
        task()
    for c in range(chunks):
        finish(c)
    for s in range(SLOTS):
        out_ref[0, s] = total[s].T.astype(jnp.bfloat16)

    for d in range(1, xs):
        table_copy(d).wait_send()
    for c in range(chunks):
        for s in range(1, half + 1):
            ring_copy(c, s, 0).wait_send()
            ring_copy(c, s, 1).wait_send()
        for d in range(1, xs):
            x_copy(c, d, 0, zs).wait_send()
        whole_sum(c).wait_send()


def on_device(xs, zs, a_blocks, a_cols, p_blocks, agg_grp, c_slot):
    rows, width, order = a_blocks.shape[:3]
    groups = lax.axis_size("grp")
    ranks = lax.axis_size("rank")
    part = order // CHUNKS
    half = zs // 2
    sizes = (xs, zs, groups, rows, width, order, CHUNKS, STAGGER)
    smem = pl.BlockSpec(memory_space=pltpu.SMEM)
    vmem = pl.BlockSpec(memory_space=pltpu.VMEM)
    dma = pltpu.SemaphoreType.DMA
    return pl.pallas_call(
        functools.partial(kernel, sizes),
        out_shape=jax.ShapeDtypeStruct((1, SLOTS, order, order), jnp.bfloat16),
        in_specs=[smem, smem, smem, vmem, pl.BlockSpec(memory_space=pl.ANY)],
        out_specs=vmem,
        scratch_shapes=[
            pltpu.VMEM((rows * width, order, order), jnp.bfloat16),
            pltpu.VMEM((CHUNKS, zs, rows, part, order), jnp.bfloat16),
            pltpu.VMEM((CHUNKS, xs - 1, zs, part, order), jnp.bfloat16),
            pltpu.VMEM((xs, 8, 128), jnp.int32),
            pltpu.VMEM((rows, SLOTS, part, order), jnp.float32),
            pltpu.VMEM((CHUNKS, groups - 1, SLOTS, part, order), jnp.bfloat16),
            pltpu.VMEM((CHUNKS, groups - 1, SLOTS, part, order), jnp.bfloat16),
            pltpu.VMEM((SLOTS, order, order), jnp.float32),
            pltpu.SMEM((xs, 8, 128), jnp.int32),
            pltpu.SMEM((rows * width,), jnp.int32),
            dma(()),
            dma(()),
            dma((xs - 1,)),
            dma((xs - 1,)),
            dma((CHUNKS, half, 2)),
            dma((CHUNKS, half, 2)),
            dma((CHUNKS, xs - 1)),
            dma((CHUNKS, xs - 1)),
            dma((CHUNKS,)),
            dma((CHUNKS,)),
        ]
        + [pltpu.VMEM((ranks + rows, part, order), jnp.bfloat16)] * CHUNKS,
        compiler_params=pltpu.CompilerParams(
            collective_id=0, has_side_effects=True, vmem_limit_bytes=40 << 20
        ),
        cost_estimate=pl.CostEstimate(
            flops=4 * rows * width * order**3,
            bytes_accessed=2 * rows * (width + 1) * order**2,
            transcendentals=0,
        ),
    )(a_cols, agg_grp, c_slot, p_blocks, a_blocks.reshape(rows * width, order, order))


def solution(mesh):
    in_specs = (
        P(("grp", "rank"), None, None, None),
        P(("grp", "rank"), None),
        P(("grp", "rank"), None, None),
        P(("grp", "rank")),
        P(("grp", "rank"), None),
    )
    out_specs = P(("grp", "rank"), None, None, None)
    return jax.shard_map(
        functools.partial(on_device, X, Z),
        mesh=mesh,
        in_specs=in_specs,
        out_specs=out_specs,
        check_vma=False,
    )
```

```python
import functools

import jax
import jax.numpy as jnp
from jax import lax
from jax.experimental import pallas as pl
from jax.experimental.pallas import tpu as pltpu
from jax.sharding import PartitionSpec as P

SLOTS = 2
CORES = 2
X = 4
Z = 12
PARTS = (32, 32, 32, 32)
OFFSETS = (0, 0.5, 1, 1.5)
AHEAD = 10
PIECES = 2
READY = 0.9
GAPS = (0.3, 0.1, 0.7)

MESH = pl.DeviceIdType.MESH
NT = (((1,), (1,)), ((), ()))


def kernel(
    sizes,
    cols_hbm,
    agg_hbm,
    slot_hbm,
    p_hbm,
    a_hbm,
    out_ref,
    cols,
    agg,
    slot,
    p_ref,
    a_ref,
    table,
    sums,
    total,
    table_smem,
    place,
    in_sem,
    table_sem,
    table_send,
    table_recv,
    ring_send,
    ring_recv,
    x_send,
    x_recv,
    sum_send,
    sum_recv,
    pair_send,
    pair_recv,
    *parted,
):
    xs, zs, groups, rows, width, order = sizes
    chunks = len(PARTS)
    firsts = [sum(PARTS[:c]) for c in range(chunks)]
    ring, stage, chosen, outgoing, incoming, pair_out, pair_in, kept = (
        parted[i * chunks : (i + 1) * chunks] for i in range(8)
    )
    ys = groups // CORES
    half = zs // 2
    ranks = xs * zs
    grp = lax.axis_index("grp")
    rank = lax.axis_index("rank")
    z, x = lax.div(rank, xs), lax.rem(rank, xs)
    y, core = lax.div(grp, CORES), lax.rem(grp, CORES)

    def rank_at(dx, dz):
        return {"rank": lax.rem(z + dz + zs, zs) * xs + lax.rem(x + dx, xs)}

    def grp_at(dy, dc=0):
        return lax.rem(y + dy, ys) * CORES + lax.rem(core + dc, CORES)

    neighbours = [rank_at(0, 1), rank_at(0, -1)]
    neighbours += [rank_at(d, 0) for d in range(1, xs)]
    neighbours += [{"grp": grp_at(dy)} for dy in range(1, ys)]
    neighbours += [{"grp": grp_at(0, 1)}]
    barrier = pltpu.get_barrier_semaphore()
    for device in neighbours:
        pl.semaphore_signal(barrier, inc=1, device_id=device, device_id_type=MESH)
    p_copy, cols_copy, agg_copy, slot_copy, a_copy = (
        pltpu.make_async_copy(source, target, in_sem.at[i])
        for i, (source, target) in enumerate(
            [(p_hbm, p_ref), (cols_hbm, cols), (agg_hbm, agg), (slot_hbm, slot), (a_hbm, a_ref)]
        )
    )
    for copy in (p_copy, cols_copy, agg_copy, slot_copy, a_copy):
        copy.start()

    p_copy.wait()
    for w in range(rows):
        turned = p_ref[w].astype(jnp.float32).T.astype(jnp.bfloat16)
        for c in range(chunks):
            ring[c][0, w] = turned[firsts[c] : firsts[c] + PARTS[c]]

    def table_copy(d):
        return pltpu.make_async_remote_copy(
            src_ref=table.at[0],
            dst_ref=table.at[xs - d],
            send_sem=table_send.at[d - 1],
            recv_sem=table_recv.at[xs - d - 1],
            device_id=rank_at(d, 0),
            device_id_type=MESH,
        )

    def ring_copy(c, s, down):
        if down:
            src, dst = (zs - s + 1) % zs, zs - s
        else:
            src, dst = s - 1, s
        source, target = ring[c].at[src], ring[c].at[dst]
        if s == half:
            which = pl.ds(down * (rows // 2), rows // 2)
            source, target = source.at[which], target.at[which]
        return pltpu.make_async_remote_copy(
            src_ref=source,
            dst_ref=target,
            send_sem=ring_send.at[c, s - 1, down],
            recv_sem=ring_recv.at[c, s - 1, down],
            device_id=rank_at(0, -1 if down else 1),
            device_id_type=MESH,
        )

    def x_copy(c, d, start, count):
        return pltpu.make_async_remote_copy(
            src_ref=stage[c].at[d - 1, pl.ds(start, count)],
            dst_ref=chosen[c].at[pl.ds((xs - d) * zs + start, count)],
            send_sem=x_send.at[c, d - 1],
            recv_sem=x_recv.at[c, xs - d - 1],
            device_id=rank_at(d, 0),
            device_id_type=MESH,
        )

    def pair_copy(c):
        return pltpu.make_async_remote_copy(
            src_ref=pair_out[c],
            dst_ref=pair_in[c],
            send_sem=pair_send.at[c],
            recv_sem=pair_recv.at[c],
            device_id={"grp": grp_at(0, 1)},
            device_id_type=MESH,
        )

    def sum_copy(c, dy):
        return pltpu.make_async_remote_copy(
            src_ref=outgoing[c].at[dy - 1],
            dst_ref=incoming[c].at[dy - 1],
            send_sem=sum_send.at[c],
            recv_sem=sum_recv.at[c],
            device_id={"grp": grp_at(dy)},
            device_id_type=MESH,
        )

    def whole_sum(c):
        return pltpu.make_async_remote_copy(
            src_ref=outgoing[c],
            dst_ref=incoming[c],
            send_sem=sum_send.at[c],
            recv_sem=sum_recv.at[c],
            device_id={"grp": grp_at(1)},
            device_id_type=MESH,
        )

    def make_tables():
        cols_copy.wait()
        lane = lax.broadcasted_iota(jnp.int32, (8, 128), 1)
        base = grp * (ranks * rows)

        def row(n, held):
            for k in range(width):
                local = cols[n, k] - base
                peer, within = lax.div(local, rows), lax.rem(local, rows)
                rx = lax.rem(lax.rem(peer, xs) - x + xs, xs)
                j = lax.rem(z - lax.div(peer, xs) + zs, zs)
                spot = jnp.where(j < half, 2 * j - 1, 2 * (zs - j))
                spot = jnp.where(j == 0, 0, jnp.where(j == half, zs - 1, spot))
                place[n * width + k] = jnp.where(
                    peer == rank, ranks + within, rx * zs + spot
                )
                held = jnp.maximum(held, jnp.where(lane == peer, within, 0))
            return held

        table[0] = lax.fori_loop(0, rows, row, jnp.zeros((8, 128), jnp.int32))
        for d in range(1, xs):
            table_copy(d).start()

    def read_tables():
        for d in range(1, xs):
            table_copy(d).wait_recv()
        fetch = pltpu.make_async_copy(table, table_smem, table_sem)
        fetch.start()
        fetch.wait()

    def pick(blocks, index):
        held = blocks[0]
        for w in range(1, rows):
            held = jnp.where(index == w, blocks[w], held)
        return held

    def own(c):
        ring_copy(c, 1, 0).start()
        ring_copy(c, 1, 1).start()

    def step(c, s):
        if s > 0:
            ring_copy(c, s, 0).wait_recv()
            ring_copy(c, s, 1).wait_recv()
            if s < half:
                ring_copy(c, s + 1, 0).start()
                ring_copy(c, s + 1, 1).start()
        if s == 0 or s == half:
            hops = [s]
        else:
            hops = [s, zs - s]
        start = 0 if s == 0 else 2 * s - 1
        for at, j in enumerate(hops):
            blocks = [ring[c][j, w] for w in range(rows)]
            spot = start + at
            source = lax.rem(z - j + zs, zs) * xs + x
            if j == 0:
                for w in range(rows):
                    chosen[c][ranks + w] = blocks[w]
                chosen[c][0] = blocks[0]
            else:
                chosen[c][spot] = pick(blocks, table_smem[0, 0, source])
            for d in range(1, xs):
                stage[c][d - 1, spot] = pick(blocks, table_smem[d, 0, source])
        for d in range(1, xs):
            x_copy(c, d, start, len(hops)).start()

    def multiply(c, piece):
        part = PARTS[c]
        if piece == 0:
            for d in range(1, xs):
                x_copy(c, d, 0, zs).wait_recv()

        def row(n, carry):
            products = []
            for k in range(width):
                q = chosen[c][place[n * width + k]]
                product = lax.dot_general(
                    q, a_ref[n * width + k], NT, preferred_element_type=jnp.float32
                )
                products.append(product.astype(jnp.bfloat16))
            term = jnp.dot(
                jnp.concatenate(products, axis=0),
                p_ref[n],
                preferred_element_type=jnp.float32,
            )
            for s in range(SLOTS):
                held = jnp.zeros((part, order), jnp.float32)
                for k in range(width):
                    mine = term[k * part : (k + 1) * part]
                    held = held + jnp.where(slot[n, k] == s, mine, 0.0)
                sums[n, s, :part] = held
            return carry

        each = rows // PIECES
        lax.fori_loop(piece * each, (piece + 1) * each, row, 0, unroll=True)

    def gather_sums(c, dy, dc, s):
        part = PARTS[c]
        held = jnp.zeros((part, order), jnp.float32)
        for n in range(rows):
            mine = agg[n] == grp_at(dy, dc)
            held = held + jnp.where(mine, sums[n, s, :part], 0.0)
        return held

    def pair_sums(c):
        for dy in range(ys):
            for s in range(SLOTS):
                pair_out[c][dy, s] = gather_sums(c, dy, 1, s).astype(jnp.bfloat16)
        pair_copy(c).start()
        for dy in range(ys):
            for s in range(SLOTS):
                kept[c][dy, s] = gather_sums(c, dy, 0, s)

    def send_sums(c):
        pair_copy(c).wait_recv()
        for dy in sorted(range(1, ys), key=lambda dy: -min(dy, ys - dy)):
            for s in range(SLOTS):
                both = kept[c][dy, s] + pair_in[c][dy, s].astype(jnp.float32)
                outgoing[c][dy - 1, s] = both.astype(jnp.bfloat16)
            sum_copy(c, dy).start()

    def finish(c):
        mine = pl.ds(firsts[c], PARTS[c])
        for s in range(SLOTS):
            total[s, mine] = kept[c][0, s] + pair_in[c][0, s].astype(jnp.float32)
        whole_sum(c).wait_recv()
        for s in range(SLOTS):
            held = total[s, mine]
            for dy in range(1, ys):
                held = held + incoming[c][dy - 1, s].astype(jnp.float32)
            total[s, mine] = held

    pl.semaphore_wait(barrier, len(neighbours))
    work = []

    def put(key, c, call, *args):
        work.append((key, len(work), call, (c, *args)))

    for c in range(chunks):
        put(OFFSETS[c] - AHEAD, c, own)
        for s in range(half + 1):
            put(OFFSETS[c] + s, c, step, s)
        key = OFFSETS[c] + half + READY
        for piece in range(PIECES):
            put(key + GAPS[0] * piece, c, multiply, piece)
        put(key + GAPS[0] + GAPS[1], c, pair_sums)
        put(key + sum(GAPS), c, send_sums)
    work.sort(key=lambda task: task[:2])
    tabled = read = False
    for key, _, call, args in work:
        if call is step and not read:
            make_tables()
            read_tables()
            read = True
        if call is multiply and not tabled:
            for copy in (agg_copy, slot_copy, a_copy):
                copy.wait()
            tabled = True
        call(*args)
    for c in range(chunks):
        finish(c)
    for s in range(SLOTS):
        out_ref[0, s] = total[s].T.astype(jnp.bfloat16)

    for d in range(1, xs):
        table_copy(d).wait_send()
    for c in range(chunks):
        for s in range(1, half + 1):
            ring_copy(c, s, 0).wait_send()
            ring_copy(c, s, 1).wait_send()
        for d in range(1, xs):
            x_copy(c, d, 0, zs).wait_send()
        pair_copy(c).wait_send()
        whole_sum(c).wait_send()


def on_device(xs, zs, a_blocks, a_cols, p_blocks, agg_grp, c_slot):
    rows, width, order = a_blocks.shape[:3]
    groups = lax.axis_size("grp")
    ys = groups // CORES
    ranks = lax.axis_size("rank")
    chunks = len(PARTS)
    half = zs // 2
    sizes = (xs, zs, groups, rows, width, order)
    dma = pltpu.SemaphoreType.DMA

    def parted(*shape, dtype=jnp.bfloat16):
        return [pltpu.VMEM((*shape, part, order), dtype) for part in PARTS]

    return pl.pallas_call(
        functools.partial(kernel, sizes),
        out_shape=jax.ShapeDtypeStruct((1, SLOTS, order, order), jnp.bfloat16),
        in_specs=[pl.BlockSpec(memory_space=pltpu.HBM)] * 5,
        out_specs=pl.BlockSpec(memory_space=pltpu.VMEM),
        scratch_shapes=[
            pltpu.SMEM((rows, width), jnp.int32),
            pltpu.SMEM((rows,), jnp.int32),
            pltpu.SMEM((rows, width), jnp.int32),
            pltpu.VMEM((rows, order, order), jnp.bfloat16),
            pltpu.VMEM((rows * width, order, order), jnp.bfloat16),
            pltpu.VMEM((xs, 8, 128), jnp.int32),
            pltpu.VMEM((rows, SLOTS, max(PARTS), order), jnp.float32),
            pltpu.VMEM((SLOTS, order, order), jnp.float32),
            pltpu.SMEM((xs, 8, 128), jnp.int32),
            pltpu.SMEM((rows * width,), jnp.int32),
            dma((5,)),
            dma(()),
            dma((xs - 1,)),
            dma((xs - 1,)),
            dma((chunks, half, 2)),
            dma((chunks, half, 2)),
            dma((chunks, xs - 1)),
            dma((chunks, xs - 1)),
            dma((chunks,)),
            dma((chunks,)),
            dma((chunks,)),
            dma((chunks,)),
        ]
        + parted(zs, rows)
        + parted(xs - 1, zs)
        + parted(ranks + rows)
        + parted(ys - 1, SLOTS)
        + parted(ys - 1, SLOTS)
        + parted(ys, SLOTS)
        + parted(ys, SLOTS)
        + parted(ys, SLOTS, dtype=jnp.float32),
        compiler_params=pltpu.CompilerParams(
            collective_id=0, has_side_effects=True, vmem_limit_bytes=62 << 20
        ),
        cost_estimate=pl.CostEstimate(
            flops=4 * rows * width * order**3,
            bytes_accessed=2 * rows * (width + 1) * order**2,
            transcendentals=0,
        ),
    )(a_cols, agg_grp, c_slot, p_blocks, a_blocks.reshape(rows * width, order, order))


def solution(mesh):
    in_specs = (
        P(("grp", "rank"), None, None, None),
        P(("grp", "rank"), None),
        P(("grp", "rank"), None, None),
        P(("grp", "rank")),
        P(("grp", "rank"), None),
    )
    out_specs = P(("grp", "rank"), None, None, None)
    return jax.shard_map(
        functools.partial(on_device, X, Z),
        mesh=mesh,
        in_specs=in_specs,
        out_specs=out_specs,
        check_vma=False,
    )
```

```python
import functools

import jax
import jax.numpy as jnp
from jax import lax
from jax.experimental import pallas as pl
from jax.experimental.pallas import tpu as pltpu
from jax.sharding import PartitionSpec as P

SLOTS = 2
CORES = 2
X = 4
Z = 12
PARTS = (32, 32, 32, 32)
OFFSETS = (0, 0.6, 1.2, 1.8)
AHEAD = 10
PIECES = 2
READY = 0.01
GAPS = (0.2, 0.2, 0.4)

MESH = pl.DeviceIdType.MESH
NT = (((1,), (1,)), ((), ()))


def kernel(
    sizes,
    cols_hbm,
    agg_hbm,
    slot_hbm,
    p_hbm,
    a_hbm,
    out_ref,
    cols,
    agg,
    slot,
    p_ref,
    a_ref,
    table,
    sums,
    total,
    table_smem,
    place,
    in_sem,
    table_sem,
    table_send,
    table_recv,
    ring_send,
    ring_recv,
    x_send,
    x_recv,
    sum_send,
    sum_recv,
    pair_send,
    pair_recv,
    far_send,
    far_recv,
    pass_send,
    pass_recv,
    late_send,
    late_recv,
    *parted,
):
    xs, zs, groups, rows, width, order = sizes
    chunks = len(PARTS)
    firsts = [sum(PARTS[:c]) for c in range(chunks)]
    ring, stage, late, passed, chosen, outgoing, incoming, pair_out, pair_in, kept = (
        parted[i * chunks : (i + 1) * chunks] for i in range(10)
    )
    ys = groups // CORES
    half = zs // 2
    full, few = half - 2, xs // 2
    early = 2 * full + 1
    ranks = xs * zs
    grp = lax.axis_index("grp")
    rank = lax.axis_index("rank")
    z, x = lax.div(rank, xs), lax.rem(rank, xs)
    y, core = lax.div(grp, CORES), lax.rem(grp, CORES)

    def rank_at(dx, dz):
        return {"rank": lax.rem(z + dz + zs, zs) * xs + lax.rem(x + dx, xs)}

    def grp_at(dy, dc=0):
        return lax.rem(y + dy, ys) * CORES + lax.rem(core + dc, CORES)

    neighbours = [rank_at(d, dz) for dz in (1, -1) for d in range(xs)]
    neighbours += [rank_at(d, 0) for d in range(1, xs)]
    neighbours += [{"grp": grp_at(dy)} for dy in range(1, ys)]
    neighbours += [{"grp": grp_at(0, 1)}]
    barrier = pltpu.get_barrier_semaphore()
    for device in neighbours:
        pl.semaphore_signal(barrier, inc=1, device_id=device, device_id_type=MESH)
    p_copy, cols_copy, agg_copy, slot_copy, a_copy = (
        pltpu.make_async_copy(source, target, in_sem.at[i])
        for i, (source, target) in enumerate(
            [(p_hbm, p_ref), (cols_hbm, cols), (agg_hbm, agg), (slot_hbm, slot), (a_hbm, a_ref)]
        )
    )
    for copy in (p_copy, cols_copy, agg_copy, slot_copy, a_copy):
        copy.start()

    p_copy.wait()
    for w in range(rows):
        turned = p_ref[w].astype(jnp.float32).T.astype(jnp.bfloat16)
        for c in range(chunks):
            ring[c][0, w] = turned[firsts[c] : firsts[c] + PARTS[c]]

    def table_copy(d):
        return pltpu.make_async_remote_copy(
            src_ref=table.at[0],
            dst_ref=table.at[xs - d],
            send_sem=table_send.at[d - 1],
            recv_sem=table_recv.at[xs - d - 1],
            device_id=rank_at(d, 0),
            device_id_type=MESH,
        )

    def ring_copy(c, s, down):
        if down:
            src, dst = (early - s + 1) % early, early - s
        else:
            src, dst = s - 1, s
        return pltpu.make_async_remote_copy(
            src_ref=ring[c].at[src],
            dst_ref=ring[c].at[dst],
            send_sem=ring_send.at[c, s - 1, down],
            recv_sem=ring_recv.at[c, s - 1, down],
            device_id=rank_at(0, -1 if down else 1),
            device_id_type=MESH,
        )

    def x_copy(c, d, start, count):
        return pltpu.make_async_remote_copy(
            src_ref=stage[c].at[d - 1, pl.ds(start, count)],
            dst_ref=chosen[c].at[pl.ds((xs - d) * early + start, count)],
            send_sem=x_send.at[c, d - 1],
            recv_sem=x_recv.at[c, xs - d - 1],
            device_id=rank_at(d, 0),
            device_id_type=MESH,
        )

    def far_copy(i):
        source, target, count = [
            (0, xs, xs),
            (0, 2 * xs, xs),
            (xs + few, 3 * xs + few, xs - few),
            (2 * xs, 3 * xs, few),
        ][i]
        return pltpu.make_async_remote_copy(
            src_ref=table.at[pl.ds(source, count)],
            dst_ref=table.at[pl.ds(target, count)],
            send_sem=far_send.at[i],
            recv_sem=far_recv.at[i],
            device_id=rank_at(0, -1 if i % 2 else 1),
            device_id_type=MESH,
        )

    def late_copy(c, down, d):
        return pltpu.make_async_remote_copy(
            src_ref=late[c].at[down * xs + d],
            dst_ref=chosen[c].at[xs * early + (xs - d) % xs * 3 + down],
            send_sem=late_send.at[c, 0],
            recv_sem=late_recv.at[c],
            device_id=rank_at(d, -1 if down else 1),
            device_id_type=MESH,
        )

    def pass_copy(c, down):
        count = xs - few if down else few
        return pltpu.make_async_remote_copy(
            src_ref=late[c].at[pl.ds(2 * xs + down * few, count)],
            dst_ref=passed[c].at[pl.ds(down * few, count)],
            send_sem=pass_send.at[c, down],
            recv_sem=pass_recv.at[c, down],
            device_id=rank_at(0, -1 if down else 1),
            device_id_type=MESH,
        )

    def last_copy(c, d):
        return pltpu.make_async_remote_copy(
            src_ref=passed[c].at[d],
            dst_ref=chosen[c].at[xs * early + (xs - d) % xs * 3 + 2],
            send_sem=late_send.at[c, 1],
            recv_sem=late_recv.at[c],
            device_id=rank_at(d, 1 if d < few else -1),
            device_id_type=MESH,
        )

    def whole_late(c, source, i):
        return pltpu.make_async_remote_copy(
            src_ref=source,
            dst_ref=chosen[c].at[pl.ds(xs * early, source.shape[0])],
            send_sem=late_send.at[c, i],
            recv_sem=late_recv.at[c],
            device_id=rank_at(0, 1),
            device_id_type=MESH,
        )

    def pair_copy(c):
        return pltpu.make_async_remote_copy(
            src_ref=pair_out[c],
            dst_ref=pair_in[c],
            send_sem=pair_send.at[c],
            recv_sem=pair_recv.at[c],
            device_id={"grp": grp_at(0, 1)},
            device_id_type=MESH,
        )

    def sum_copy(c, dy):
        return pltpu.make_async_remote_copy(
            src_ref=outgoing[c].at[dy - 1],
            dst_ref=incoming[c].at[dy - 1],
            send_sem=sum_send.at[c],
            recv_sem=sum_recv.at[c],
            device_id={"grp": grp_at(dy)},
            device_id_type=MESH,
        )

    def whole_sum(c):
        return pltpu.make_async_remote_copy(
            src_ref=outgoing[c],
            dst_ref=incoming[c],
            send_sem=sum_send.at[c],
            recv_sem=sum_recv.at[c],
            device_id={"grp": grp_at(1)},
            device_id_type=MESH,
        )

    def make_tables():
        cols_copy.wait()
        lane = lax.broadcasted_iota(jnp.int32, (1, 128), 1)
        base = grp * (ranks * rows)

        def row(n, held):
            for k in range(width):
                local = cols[n, k] - base
                peer, within = lax.div(local, rows), lax.rem(local, rows)
                rx = lax.rem(lax.rem(peer, xs) - x + xs, xs)
                j = lax.rem(z - lax.div(peer, xs) + zs, zs)
                spot = jnp.where(j < half, 2 * j - 1, 2 * (zs - j))
                spot = jnp.where(j == half, zs - 1, jnp.maximum(spot, 0))
                spot = jnp.where(
                    spot < early,
                    rx * early + spot,
                    xs * early + rx * 3 + spot - early,
                )
                place[n * width + k] = jnp.where(peer == rank, ranks + within, spot)
                held = jnp.maximum(held, jnp.where(lane == peer, within, 0))
            return held

        table[0] = lax.fori_loop(0, rows, row, jnp.zeros((1, 128), jnp.int32))
        for d in range(1, xs):
            table_copy(d).start()

    def read_tables():
        for d in range(1, xs):
            table_copy(d).wait_recv()
        far_copy(0).start()
        far_copy(1).start()
        fetch_tables(0, xs)

    def fetch_tables(start, count):
        which = pl.ds(start, count)
        fetch = pltpu.make_async_copy(table.at[which], table_smem.at[which], table_sem)
        fetch.start()
        fetch.wait()

    def pass_tables():
        far_copy(0).wait_recv()
        far_copy(1).wait_recv()
        far_copy(2).start()
        far_copy(3).start()

    def read_far_tables():
        far_copy(2).wait_recv()
        far_copy(3).wait_recv()
        fetch_tables(xs, 3 * xs)

    def pick(blocks, index):
        held = blocks[0]
        for w in range(1, rows):
            held = jnp.where(index == w, blocks[w], held)
        return held

    def own(c):
        ring_copy(c, 1, 0).start()
        ring_copy(c, 1, 1).start()

    def send_late(c, down):
        j = half + 2 if down else full
        source = lax.rem(z - j + zs, zs) * xs + x
        blocks = [ring[c][early - full if down else full, w] for w in range(rows)]
        passing = range(few, xs) if down else range(few)
        for d in passing:
            late[c][2 * xs + d] = pick(blocks, table_smem[3 * xs + d, 0, source])
        pass_copy(c, down).start()
        for d in range(xs):
            index = table_smem[(1 if down else 2) * xs + d, 0, source]
            late[c][down * xs + d] = pick(blocks, index)
            late_copy(c, down, d).start()

    def step(c, s):
        if s == full + 1:
            for down in (0, 1):
                pass_copy(c, down).wait_recv()
                for d in range(few, xs) if down else range(few):
                    last_copy(c, d).start()
            return
        if s > 0:
            ring_copy(c, s, 0).wait_recv()
            ring_copy(c, s, 1).wait_recv()
        if s == full:
            send_late(c, 0)
            send_late(c, 1)
        elif s > 0:
            ring_copy(c, s + 1, 0).start()
            ring_copy(c, s + 1, 1).start()
        hops = [(0, 0)] if s == 0 else [(s, s), (zs - s, early - s)]
        start = 0 if s == 0 else 2 * s - 1
        for at, (j, held) in enumerate(hops):
            blocks = [ring[c][held, w] for w in range(rows)]
            spot = start + at
            source = lax.rem(z - j + zs, zs) * xs + x
            if j == 0:
                for w in range(rows):
                    chosen[c][ranks + w] = blocks[w]
                chosen[c][0] = blocks[0]
            else:
                chosen[c][spot] = pick(blocks, table_smem[0, 0, source])
            for d in range(1, xs):
                stage[c][d - 1, spot] = pick(blocks, table_smem[d, 0, source])
        for d in range(1, xs):
            x_copy(c, d, start, len(hops)).start()

    def multiply(c, piece):
        part = PARTS[c]
        if piece == 0:
            for d in range(1, xs):
                x_copy(c, d, 0, early).wait_recv()
            whole_late(c, late[c], 0).wait_recv()

        def row(n, carry):
            products = []
            for k in range(width):
                q = chosen[c][place[n * width + k]]
                product = lax.dot_general(
                    q, a_ref[n * width + k], NT, preferred_element_type=jnp.float32
                )
                products.append(product.astype(jnp.bfloat16))
            term = jnp.dot(
                jnp.concatenate(products, axis=0),
                p_ref[n],
                preferred_element_type=jnp.float32,
            )
            for s in range(SLOTS):
                held = jnp.zeros((part, order), jnp.float32)
                for k in range(width):
                    mine = term[k * part : (k + 1) * part]
                    held = held + jnp.where(slot[n, k] == s, mine, 0.0)
                sums[n, s, :part] = held
            return carry

        each = rows // PIECES
        lax.fori_loop(piece * each, (piece + 1) * each, row, 0, unroll=True)

    def gather_sums(c, dy, dc, s):
        part = PARTS[c]
        held = jnp.zeros((part, order), jnp.float32)
        for n in range(rows):
            mine = agg[n] == grp_at(dy, dc)
            held = held + jnp.where(mine, sums[n, s, :part], 0.0)
        return held

    def pair_sums(c):
        for dy in range(ys):
            for s in range(SLOTS):
                pair_out[c][dy, s] = gather_sums(c, dy, 1, s).astype(jnp.bfloat16)
        pair_copy(c).start()
        for dy in range(ys):
            for s in range(SLOTS):
                kept[c][dy, s] = gather_sums(c, dy, 0, s)

    def send_sums(c):
        pair_copy(c).wait_recv()
        for dy in sorted(range(1, ys), key=lambda dy: -min(dy, ys - dy)):
            for s in range(SLOTS):
                both = kept[c][dy, s] + pair_in[c][dy, s].astype(jnp.float32)
                outgoing[c][dy - 1, s] = both.astype(jnp.bfloat16)
            sum_copy(c, dy).start()

    def finish(c):
        mine = pl.ds(firsts[c], PARTS[c])
        for s in range(SLOTS):
            total[s, mine] = kept[c][0, s] + pair_in[c][0, s].astype(jnp.float32)
        whole_sum(c).wait_recv()
        for s in range(SLOTS):
            held = total[s, mine]
            for dy in range(1, ys):
                held = held + incoming[c][dy - 1, s].astype(jnp.float32)
            total[s, mine] = held

    pl.semaphore_wait(barrier, len(neighbours))
    work = []

    def put(key, c, call, *args):
        work.append((key, len(work), call, (c, *args)))

    for c in range(chunks):
        put(OFFSETS[c] - AHEAD, c, own)
        for s in range(half):
            put(OFFSETS[c] + s, c, step, s)
        key = OFFSETS[c] + half + READY
        for piece in range(PIECES):
            put(key + GAPS[0] * piece, c, multiply, piece)
        put(key + GAPS[0] + GAPS[1], c, pair_sums)
        put(key + sum(GAPS), c, send_sums)
    work.append((full * 0.4, len(work), pass_tables, ()))
    work.append((full * 0.9, len(work), read_far_tables, ()))
    work.sort(key=lambda task: task[:2])
    tabled = read = False
    for key, _, call, args in work:
        if call is step and not read:
            make_tables()
            read_tables()
            read = True
        if call is multiply and not tabled:
            for copy in (agg_copy, slot_copy, a_copy):
                copy.wait()
            tabled = True
        call(*args)
    for c in range(chunks):
        finish(c)
    for s in range(SLOTS):
        out_ref[0, s] = total[s].T.astype(jnp.bfloat16)

    for d in range(1, xs):
        table_copy(d).wait_send()
    for i in range(4):
        far_copy(i).wait_send()
    for c in range(chunks):
        for s in range(1, full + 1):
            ring_copy(c, s, 0).wait_send()
            ring_copy(c, s, 1).wait_send()
        for d in range(1, xs):
            x_copy(c, d, 0, early).wait_send()
        whole_late(c, late[c].at[pl.ds(0, 2 * xs)], 0).wait_send()
        whole_late(c, passed[c], 1).wait_send()
        for down in (0, 1):
            pass_copy(c, down).wait_send()
        pair_copy(c).wait_send()
        whole_sum(c).wait_send()


def on_device(xs, zs, a_blocks, a_cols, p_blocks, agg_grp, c_slot):
    rows, width, order = a_blocks.shape[:3]
    groups = lax.axis_size("grp")
    ys = groups // CORES
    ranks = lax.axis_size("rank")
    chunks = len(PARTS)
    full = zs // 2 - 2
    early = 2 * full + 1
    sizes = (xs, zs, groups, rows, width, order)
    dma = pltpu.SemaphoreType.DMA

    def parted(*shape, dtype=jnp.bfloat16):
        return [pltpu.VMEM((*shape, part, order), dtype) for part in PARTS]

    return pl.pallas_call(
        functools.partial(kernel, sizes),
        out_shape=pltpu.VMEM((1, SLOTS, order, order), jnp.bfloat16),
        in_specs=[pl.BlockSpec(memory_space=pltpu.HBM)] * 5,
        out_specs=pl.BlockSpec(memory_space=pltpu.VMEM),
        scratch_shapes=[
            pltpu.SMEM((rows, width), jnp.int32),
            pltpu.SMEM((rows,), jnp.int32),
            pltpu.SMEM((rows, width), jnp.int32),
            pltpu.VMEM((rows, order, order), jnp.bfloat16),
            pltpu.VMEM((rows * width, order, order), jnp.bfloat16),
            pltpu.VMEM((4 * xs, 1, 128), jnp.int32),
            pltpu.VMEM((rows, SLOTS, max(PARTS), order), jnp.float32),
            pltpu.VMEM((SLOTS, order, order), jnp.float32),
            pltpu.SMEM((4 * xs, 1, 128), jnp.int32),
            pltpu.SMEM((rows * width,), jnp.int32),
            dma((5,)),
            dma(()),
            dma((xs - 1,)),
            dma((xs - 1,)),
            dma((chunks, full, 2)),
            dma((chunks, full, 2)),
            dma((chunks, xs - 1)),
            dma((chunks, xs - 1)),
            dma((chunks,)),
            dma((chunks,)),
            dma((chunks,)),
            dma((chunks,)),
            dma((4,)),
            dma((4,)),
            dma((chunks, 2)),
            dma((chunks, 2)),
            dma((chunks, 2)),
            dma((chunks,)),
        ]
        + parted(early, rows)
        + parted(xs - 1, early)
        + parted(3 * xs)
        + parted(xs)
        + parted(ranks + rows)
        + parted(ys - 1, SLOTS)
        + parted(ys - 1, SLOTS)
        + parted(ys, SLOTS)
        + parted(ys, SLOTS)
        + parted(ys, SLOTS, dtype=jnp.float32),
        compiler_params=pltpu.CompilerParams(
            collective_id=0, has_side_effects=True, vmem_limit_bytes=62 << 20
        ),
        cost_estimate=pl.CostEstimate(
            flops=4 * rows * width * order**3,
            bytes_accessed=2 * rows * (width + 1) * order**2,
            transcendentals=0,
        ),
    )(a_cols, agg_grp, c_slot, p_blocks, a_blocks.reshape(rows * width, order, order))


def solution(mesh):
    in_specs = (
        P(("grp", "rank"), None, None, None),
        P(("grp", "rank"), None),
        P(("grp", "rank"), None, None),
        P(("grp", "rank")),
        P(("grp", "rank"), None),
    )
    out_specs = P(("grp", "rank"), None, None, None)
    return jax.shard_map(
        functools.partial(on_device, X, Z),
        mesh=mesh,
        in_specs=in_specs,
        out_specs=out_specs,
        check_vma=False,
    )
```

```python
import functools

import jax
import jax.numpy as jnp
from jax import lax
from jax.experimental import pallas as pl
from jax.experimental.pallas import tpu as pltpu
from jax.sharding import PartitionSpec as P

SLOTS = 2
CORES = 2
X = 4
Z = 12
PARTS = (32, 32, 32, 32)
LAG = 0
LAG_GROWTH = 0.15
AHEAD = 10
TURN = 0.08
PIECES = 2
READY = 0.01
GAPS = (0.2, 0.2, 0.4)

MESH = pl.DeviceIdType.MESH


def kernel(
    sizes,
    cols_hbm,
    agg_hbm,
    slot_hbm,
    p_hbm,
    a_hbm,
    out_ref,
    cols,
    agg,
    slot,
    p_ref,
    a_ref,
    table,
    sums,
    total,
    table_smem,
    place,
    in_sem,
    table_sem,
    table_send,
    table_recv,
    ring_send,
    ring_recv,
    x_send,
    x_recv,
    sum_send,
    sum_recv,
    pair_send,
    pair_recv,
    far_send,
    far_recv,
    pass_send,
    pass_recv,
    late_send,
    late_recv,
    *parted,
):
    xs, zs, groups, rows, width, order = sizes
    chunks = len(PARTS)
    firsts = [sum(PARTS[:c]) for c in range(chunks)]
    ring, stage, late, passed, chosen, outgoing, incoming, pair_out, pair_in, kept = (
        parted[i * chunks : (i + 1) * chunks] for i in range(10)
    )
    ys = groups // CORES
    half = zs // 2
    full, few = half - 2, xs // 2
    early = 2 * full + 1
    ranks = xs * zs
    grp = lax.axis_index("grp")
    rank = lax.axis_index("rank")
    z, x = lax.div(rank, xs), lax.rem(rank, xs)
    y, core = lax.div(grp, CORES), lax.rem(grp, CORES)

    def rank_at(dx, dz):
        return {"rank": lax.rem(z + dz + zs, zs) * xs + lax.rem(x + dx, xs)}

    def grp_at(dy, dc=0):
        return lax.rem(y + dy, ys) * CORES + lax.rem(core + dc, CORES)

    neighbours = [rank_at(d, dz) for dz in (1, -1) for d in range(xs)]
    neighbours += [rank_at(d, 0) for d in range(1, xs)]
    neighbours += [{"grp": grp_at(dy)} for dy in range(1, ys)]
    neighbours += [{"grp": grp_at(0, 1)}]
    barrier = pltpu.get_barrier_semaphore()
    for device in neighbours:
        pl.semaphore_signal(barrier, inc=1, device_id=device, device_id_type=MESH)
    p_copy, cols_copy, agg_copy, slot_copy, a_copy = (
        pltpu.make_async_copy(source, target, in_sem.at[i])
        for i, (source, target) in enumerate(
            [(p_hbm, p_ref), (cols_hbm, cols), (agg_hbm, agg), (slot_hbm, slot), (a_hbm, a_ref)]
        )
    )
    for copy in (p_copy, cols_copy, agg_copy, slot_copy, a_copy):
        copy.start()

    p_copy.wait()
    for w in range(rows):
        turned = p_ref[w].astype(jnp.float32).T.astype(jnp.bfloat16)
        for c in range(chunks):
            ring[c][0, w] = turned[firsts[c] : firsts[c] + PARTS[c]]

    def table_copy(d):
        return pltpu.make_async_remote_copy(
            src_ref=table.at[0],
            dst_ref=table.at[xs - d],
            send_sem=table_send.at[d - 1],
            recv_sem=table_recv.at[xs - d - 1],
            device_id=rank_at(d, 0),
            device_id_type=MESH,
        )

    def ring_copy(c, s, down):
        if down:
            src, dst = (early - s + 1) % early, early - s
        else:
            src, dst = s - 1, s
        return pltpu.make_async_remote_copy(
            src_ref=ring[c].at[src],
            dst_ref=ring[c].at[dst],
            send_sem=ring_send.at[c, s - 1, down],
            recv_sem=ring_recv.at[c, s - 1, down],
            device_id=rank_at(0, -1 if down else 1),
            device_id_type=MESH,
        )

    def x_copy(c, d, start, count):
        return pltpu.make_async_remote_copy(
            src_ref=stage[c].at[d - 1, pl.ds(start, count)],
            dst_ref=chosen[c].at[pl.ds((xs - d) * early + start, count)],
            send_sem=x_send.at[c, d - 1],
            recv_sem=x_recv.at[c, xs - d - 1],
            device_id=rank_at(d, 0),
            device_id_type=MESH,
        )

    def far_copy(i):
        source, target, count = [
            (0, xs, xs),
            (0, 2 * xs, xs),
            (xs + few, 3 * xs + few, xs - few),
            (2 * xs, 3 * xs, few),
        ][i]
        return pltpu.make_async_remote_copy(
            src_ref=table.at[pl.ds(source, count)],
            dst_ref=table.at[pl.ds(target, count)],
            send_sem=far_send.at[i],
            recv_sem=far_recv.at[i],
            device_id=rank_at(0, -1 if i % 2 else 1),
            device_id_type=MESH,
        )

    def late_copy(c, down, d):
        return pltpu.make_async_remote_copy(
            src_ref=late[c].at[down * xs + d],
            dst_ref=chosen[c].at[xs * early + (xs - d) % xs * 3 + down],
            send_sem=late_send.at[c, 0],
            recv_sem=late_recv.at[c],
            device_id=rank_at(d, -1 if down else 1),
            device_id_type=MESH,
        )

    def pass_copy(c, down):
        count = xs - few if down else few
        return pltpu.make_async_remote_copy(
            src_ref=late[c].at[pl.ds(2 * xs + down * few, count)],
            dst_ref=passed[c].at[pl.ds(down * few, count)],
            send_sem=pass_send.at[c, down],
            recv_sem=pass_recv.at[c, down],
            device_id=rank_at(0, -1 if down else 1),
            device_id_type=MESH,
        )

    def last_copy(c, d):
        return pltpu.make_async_remote_copy(
            src_ref=passed[c].at[d],
            dst_ref=chosen[c].at[xs * early + (xs - d) % xs * 3 + 2],
            send_sem=late_send.at[c, 1],
            recv_sem=late_recv.at[c],
            device_id=rank_at(d, 1 if d < few else -1),
            device_id_type=MESH,
        )

    def whole_late(c, source, i):
        return pltpu.make_async_remote_copy(
            src_ref=source,
            dst_ref=chosen[c].at[pl.ds(xs * early, source.shape[0])],
            send_sem=late_send.at[c, i],
            recv_sem=late_recv.at[c],
            device_id=rank_at(0, 1),
            device_id_type=MESH,
        )

    def pair_copy(c):
        return pltpu.make_async_remote_copy(
            src_ref=pair_out[c],
            dst_ref=pair_in[c],
            send_sem=pair_send.at[c],
            recv_sem=pair_recv.at[c],
            device_id={"grp": grp_at(0, 1)},
            device_id_type=MESH,
        )

    def sum_copy(c, dy):
        return pltpu.make_async_remote_copy(
            src_ref=outgoing[c].at[dy - 1],
            dst_ref=incoming[c].at[dy - 1],
            send_sem=sum_send.at[c],
            recv_sem=sum_recv.at[c],
            device_id={"grp": grp_at(dy)},
            device_id_type=MESH,
        )

    def whole_sum(c):
        return pltpu.make_async_remote_copy(
            src_ref=outgoing[c],
            dst_ref=incoming[c],
            send_sem=sum_send.at[c],
            recv_sem=sum_recv.at[c],
            device_id={"grp": grp_at(1)},
            device_id_type=MESH,
        )

    def make_tables():
        cols_copy.wait()
        lane = lax.broadcasted_iota(jnp.int32, (1, 128), 1)
        base = grp * (ranks * rows)

        def row(n, held):
            for k in range(width):
                local = cols[n, k] - base
                peer, within = lax.div(local, rows), lax.rem(local, rows)
                rx = lax.rem(lax.rem(peer, xs) - x + xs, xs)
                j = lax.rem(z - lax.div(peer, xs) + zs, zs)
                spot = jnp.where(j < half, 2 * j - 1, 2 * (zs - j))
                spot = jnp.where(j == half, zs - 1, jnp.maximum(spot, 0))
                spot = jnp.where(
                    spot < early,
                    rx * early + spot,
                    xs * early + rx * 3 + spot - early,
                )
                place[n * width + k] = jnp.where(peer == rank, ranks + within, spot)
                held = jnp.maximum(held, jnp.where(lane == peer, within, 0))
            return held

        table[0] = lax.fori_loop(0, rows, row, jnp.zeros((1, 128), jnp.int32))
        for d in range(1, xs):
            table_copy(d).start()

    def read_tables():
        for d in range(1, xs):
            table_copy(d).wait_recv()
        far_copy(0).start()
        far_copy(1).start()
        fetch_tables(0, xs)

    def fetch_tables(start, count):
        which = pl.ds(start, count)
        fetch = pltpu.make_async_copy(table.at[which], table_smem.at[which], table_sem)
        fetch.start()
        fetch.wait()

    def pass_tables():
        far_copy(0).wait_recv()
        far_copy(1).wait_recv()
        far_copy(2).start()
        far_copy(3).start()

    def read_far_tables():
        far_copy(2).wait_recv()
        far_copy(3).wait_recv()
        fetch_tables(xs, 3 * xs)

    def pick(blocks, index):
        held = blocks[0]
        for w in range(1, rows):
            held = jnp.where(index == w, blocks[w], held)
        return held

    def own(c):
        ring_copy(c, 1, 0).start()
        ring_copy(c, 1, 1).start()

    def send_late(c, down):
        j = half + 2 if down else full
        source = lax.rem(z - j + zs, zs) * xs + x
        blocks = [ring[c][early - full if down else full, w] for w in range(rows)]
        passing = range(few, xs) if down else range(few)
        for d in passing:
            late[c][2 * xs + d] = pick(blocks, table_smem[3 * xs + d, 0, source])
        pass_copy(c, down).start()
        for d in range(xs):
            index = table_smem[(1 if down else 2) * xs + d, 0, source]
            late[c][down * xs + d] = pick(blocks, index)
            late_copy(c, down, d).start()

    def step(c, s):
        if s == full + 1:
            for down in (0, 1):
                pass_copy(c, down).wait_recv()
                for d in range(few, xs) if down else range(few):
                    last_copy(c, d).start()
            return
        if s > 0:
            ring_copy(c, s, 0).wait_recv()
            ring_copy(c, s, 1).wait_recv()
        if s == full:
            send_late(c, 0)
            send_late(c, 1)
        elif s > 0:
            ring_copy(c, s + 1, 0).start()
            ring_copy(c, s + 1, 1).start()
        hops = [(0, 0)] if s == 0 else [(s, s), (zs - s, early - s)]
        start = 0 if s == 0 else 2 * s - 1
        for at, (j, held) in enumerate(hops):
            blocks = [ring[c][held, w] for w in range(rows)]
            spot = start + at
            source = lax.rem(z - j + zs, zs) * xs + x
            if j == 0:
                for w in range(rows):
                    chosen[c][ranks + w] = blocks[w]
                chosen[c][0] = blocks[0]
            else:
                chosen[c][spot] = pick(blocks, table_smem[0, 0, source])
            for d in range(1, xs):
                stage[c][d - 1, spot] = pick(blocks, table_smem[d, 0, source])
        for d in range(1, xs):
            x_copy(c, d, start, len(hops)).start()

    def turn(n):
        if n == 0:
            a_copy.wait()

        def block(e, carry):
            a_ref[e] = a_ref[e].T
            return carry

        lax.fori_loop(n * width, (n + 1) * width, block, 0, unroll=4)

    def multiply(c, piece):
        part = PARTS[c]
        if piece == 0:
            for d in range(1, xs):
                x_copy(c, d, 0, early).wait_recv()
            whole_late(c, late[c], 0).wait_recv()

        def row(n, carry):
            products = []
            for k in range(width):
                q = chosen[c][place[n * width + k]]
                product = jnp.dot(
                    q, a_ref[n * width + k], preferred_element_type=jnp.float32
                )
                products.append(product.astype(jnp.bfloat16))
            term = jnp.dot(
                jnp.concatenate(products, axis=0),
                p_ref[n],
                preferred_element_type=jnp.float32,
            )
            for s in range(SLOTS):
                held = jnp.zeros((part, order), jnp.float32)
                for k in range(width):
                    mine = term[k * part : (k + 1) * part]
                    held = held + jnp.where(slot[n, k] == s, mine, 0.0)
                sums[n, s, :part] = held
            return carry

        each = rows // PIECES
        lax.fori_loop(piece * each, (piece + 1) * each, row, 0, unroll=True)

    def gather_sums(c, dy, dc, s):
        part = PARTS[c]
        held = jnp.zeros((part, order), jnp.float32)
        for n in range(rows):
            mine = agg[n] == grp_at(dy, dc)
            held = held + jnp.where(mine, sums[n, s, :part], 0.0)
        return held

    def pair_sums(c):
        for dy in range(ys):
            for s in range(SLOTS):
                pair_out[c][dy, s] = gather_sums(c, dy, 1, s).astype(jnp.bfloat16)
        pair_copy(c).start()
        for dy in range(ys):
            for s in range(SLOTS):
                kept[c][dy, s] = gather_sums(c, dy, 0, s)

    def send_sums(c):
        pair_copy(c).wait_recv()
        for dy in sorted(range(1, ys), key=lambda dy: -min(dy, ys - dy)):
            for s in range(SLOTS):
                both = kept[c][dy, s] + pair_in[c][dy, s].astype(jnp.float32)
                outgoing[c][dy - 1, s] = both.astype(jnp.bfloat16)
            sum_copy(c, dy).start()

    def finish(c):
        mine = pl.ds(firsts[c], PARTS[c])
        for s in range(SLOTS):
            total[s, mine] = kept[c][0, s] + pair_in[c][0, s].astype(jnp.float32)
        whole_sum(c).wait_recv()
        for s in range(SLOTS):
            held = total[s, mine]
            for dy in range(1, ys):
                held = held + incoming[c][dy - 1, s].astype(jnp.float32)
            total[s, mine] = held

    pl.semaphore_wait(barrier, len(neighbours))
    work = []

    def put(hop, c, call, *args):
        key = hop + c * (LAG + LAG_GROWTH * min(max(hop, 0), half))
        work.append((key, len(work), call, (c, *args)))

    for c in range(chunks):
        put(-AHEAD, c, own)
        for s in range(half):
            put(s, c, step, s)
        key = half + READY
        for piece in range(PIECES):
            put(key + GAPS[0] * piece, c, multiply, piece)
        put(key + GAPS[0] + GAPS[1], c, pair_sums)
        put(key + sum(GAPS), c, send_sums)
    for n in range(rows):
        work.append((full * (0.2 + TURN * n), len(work), turn, (n,)))
    work.append((full * 0.4, len(work), pass_tables, ()))
    work.append((full * 0.9, len(work), read_far_tables, ()))
    work.sort(key=lambda task: task[:2])
    tabled = read = False
    for key, _, call, args in work:
        if call is step and not read:
            make_tables()
            read_tables()
            read = True
        if call is multiply and not tabled:
            for copy in (agg_copy, slot_copy):
                copy.wait()
            tabled = True
        call(*args)
    for c in range(chunks):
        finish(c)
    for s in range(SLOTS):
        out_ref[0, s] = total[s].T.astype(jnp.bfloat16)

    for d in range(1, xs):
        table_copy(d).wait_send()
    for i in range(4):
        far_copy(i).wait_send()
    for c in range(chunks):
        for s in range(1, full + 1):
            ring_copy(c, s, 0).wait_send()
            ring_copy(c, s, 1).wait_send()
        for d in range(1, xs):
            x_copy(c, d, 0, early).wait_send()
        whole_late(c, late[c].at[pl.ds(0, 2 * xs)], 0).wait_send()
        whole_late(c, passed[c], 1).wait_send()
        for down in (0, 1):
            pass_copy(c, down).wait_send()
        pair_copy(c).wait_send()
        whole_sum(c).wait_send()


def on_device(xs, zs, a_blocks, a_cols, p_blocks, agg_grp, c_slot):
    rows, width, order = a_blocks.shape[:3]
    groups = lax.axis_size("grp")
    ys = groups // CORES
    ranks = lax.axis_size("rank")
    chunks = len(PARTS)
    full = zs // 2 - 2
    early = 2 * full + 1
    sizes = (xs, zs, groups, rows, width, order)
    dma = pltpu.SemaphoreType.DMA

    def parted(*shape, dtype=jnp.bfloat16):
        return [pltpu.VMEM((*shape, part, order), dtype) for part in PARTS]

    return pl.pallas_call(
        functools.partial(kernel, sizes),
        out_shape=pltpu.VMEM((1, SLOTS, order, order), jnp.bfloat16),
        in_specs=[pl.BlockSpec(memory_space=pltpu.HBM)] * 5,
        out_specs=pl.BlockSpec(memory_space=pltpu.VMEM),
        scratch_shapes=[
            pltpu.SMEM((rows, width), jnp.int32),
            pltpu.SMEM((rows,), jnp.int32),
            pltpu.SMEM((rows, width), jnp.int32),
            pltpu.VMEM((rows, order, order), jnp.bfloat16),
            pltpu.VMEM((rows * width, order, order), jnp.bfloat16),
            pltpu.VMEM((4 * xs, 1, 128), jnp.int32),
            pltpu.VMEM((rows, SLOTS, max(PARTS), order), jnp.float32),
            pltpu.VMEM((SLOTS, order, order), jnp.float32),
            pltpu.SMEM((4 * xs, 1, 128), jnp.int32),
            pltpu.SMEM((rows * width,), jnp.int32),
            dma((5,)),
            dma(()),
            dma((xs - 1,)),
            dma((xs - 1,)),
            dma((chunks, full, 2)),
            dma((chunks, full, 2)),
            dma((chunks, xs - 1)),
            dma((chunks, xs - 1)),
            dma((chunks,)),
            dma((chunks,)),
            dma((chunks,)),
            dma((chunks,)),
            dma((4,)),
            dma((4,)),
            dma((chunks, 2)),
            dma((chunks, 2)),
            dma((chunks, 2)),
            dma((chunks,)),
        ]
        + parted(early, rows)
        + parted(xs - 1, early)
        + parted(3 * xs)
        + parted(xs)
        + parted(ranks + rows)
        + parted(ys - 1, SLOTS)
        + parted(ys - 1, SLOTS)
        + parted(ys, SLOTS)
        + parted(ys, SLOTS)
        + parted(ys, SLOTS, dtype=jnp.float32),
        compiler_params=pltpu.CompilerParams(
            collective_id=0, has_side_effects=True, vmem_limit_bytes=62 << 20
        ),
        cost_estimate=pl.CostEstimate(
            flops=4 * rows * width * order**3,
            bytes_accessed=2 * rows * (width + 1) * order**2,
            transcendentals=0,
        ),
    )(a_cols, agg_grp, c_slot, p_blocks, a_blocks.reshape(rows * width, order, order))


def solution(mesh):
    in_specs = (
        P(("grp", "rank"), None, None, None),
        P(("grp", "rank"), None),
        P(("grp", "rank"), None, None),
        P(("grp", "rank")),
        P(("grp", "rank"), None),
    )
    out_specs = P(("grp", "rank"), None, None, None)
    return jax.shard_map(
        functools.partial(on_device, X, Z),
        mesh=mesh,
        in_specs=in_specs,
        out_specs=out_specs,
        check_vma=False,
    )
```

```python
import functools

import jax
import jax.numpy as jnp
from jax import lax
from jax.experimental import pallas as pl
from jax.experimental.pallas import tpu as pltpu
from jax.sharding import PartitionSpec as P

SLOTS = 2
CORES = 2
X = 4
Z = 12
PARTS = (32, 32, 32, 32)
LAG = 0
LAG_GROWTH = 0.15
AHEAD = 10
TURN = 0.08
PIECES = 2
READY = 0.01
GAPS = (0.2, 0.2, 0.4)

MESH = pl.DeviceIdType.MESH


def kernel(
    sizes,
    cols_hbm,
    agg_hbm,
    slot_hbm,
    p_hbm,
    a_hbm,
    out_ref,
    cols,
    agg,
    slot,
    p_ref,
    a_ref,
    table,
    sums,
    total,
    table_smem,
    place,
    in_sem,
    table_sem,
    table_send,
    table_recv,
    ring_send,
    ring_recv,
    x_send,
    x_recv,
    sum_send,
    sum_recv,
    pair_send,
    pair_recv,
    far_send,
    far_recv,
    pass_send,
    pass_recv,
    late_send,
    late_recv,
    *parted,
):
    xs, zs, groups, rows, width, order = sizes
    chunks = len(PARTS)
    firsts = [sum(PARTS[:c]) for c in range(chunks)]
    ring, stage, late, passed, chosen, outgoing, incoming, pair_out, pair_in, kept = (
        parted[i * chunks : (i + 1) * chunks] for i in range(10)
    )
    ys = groups // CORES
    half = zs // 2
    full, few = half - 2, xs // 2
    early = 2 * full + 1
    ranks = xs * zs
    grp = lax.axis_index("grp")
    rank = lax.axis_index("rank")
    z, x = lax.div(rank, xs), lax.rem(rank, xs)
    y, core = lax.div(grp, CORES), lax.rem(grp, CORES)

    def rank_at(dx, dz):
        return {"rank": lax.rem(z + dz + zs, zs) * xs + lax.rem(x + dx, xs)}

    def grp_at(dy, dc=0):
        return lax.rem(y + dy, ys) * CORES + lax.rem(core + dc, CORES)

    neighbours = [rank_at(d, dz) for dz in (1, -1) for d in range(xs)]
    neighbours += [rank_at(d, 0) for d in range(1, xs)]
    neighbours += [{"grp": grp_at(dy)} for dy in range(1, ys)]
    neighbours += [{"grp": grp_at(0, 1)}]
    barrier = pltpu.get_barrier_semaphore()
    for device in neighbours:
        pl.semaphore_signal(barrier, inc=1, device_id=device, device_id_type=MESH)
    p_copy, cols_copy, agg_copy, slot_copy, a_copy = (
        pltpu.make_async_copy(source, target, in_sem.at[i])
        for i, (source, target) in enumerate(
            [(p_hbm, p_ref), (cols_hbm, cols), (agg_hbm, agg), (slot_hbm, slot), (a_hbm, a_ref)]
        )
    )
    for copy in (p_copy, cols_copy, agg_copy, slot_copy, a_copy):
        copy.start()

    p_copy.wait()
    for w in range(rows):
        turned = p_ref[w].astype(jnp.float32).T.astype(jnp.bfloat16)
        for c in range(chunks):
            ring[c][0, w] = turned[firsts[c] : firsts[c] + PARTS[c]]

    def table_copy(d):
        return pltpu.make_async_remote_copy(
            src_ref=table.at[0],
            dst_ref=table.at[xs - d],
            send_sem=table_send.at[d - 1],
            recv_sem=table_recv.at[xs - d - 1],
            device_id=rank_at(d, 0),
            device_id_type=MESH,
        )

    def ring_copy(c, s, down):
        if down:
            src, dst = (early - s + 1) % early, early - s
        else:
            src, dst = s - 1, s
        return pltpu.make_async_remote_copy(
            src_ref=ring[c].at[src],
            dst_ref=ring[c].at[dst],
            send_sem=ring_send.at[c, s - 1, down],
            recv_sem=ring_recv.at[c, s - 1, down],
            device_id=rank_at(0, -1 if down else 1),
            device_id_type=MESH,
        )

    def x_copy(c, d, start, count):
        return pltpu.make_async_remote_copy(
            src_ref=stage[c].at[d - 1, pl.ds(start, count)],
            dst_ref=chosen[c].at[pl.ds((xs - d) * early + start, count)],
            send_sem=x_send.at[c, d - 1],
            recv_sem=x_recv.at[c, xs - d - 1],
            device_id=rank_at(d, 0),
            device_id_type=MESH,
        )

    def far_copy(i):
        source, target, count = [
            (0, xs, xs),
            (0, 2 * xs, xs),
            (xs + few, 3 * xs + few, xs - few),
            (2 * xs, 3 * xs, few),
        ][i]
        return pltpu.make_async_remote_copy(
            src_ref=table.at[pl.ds(source, count)],
            dst_ref=table.at[pl.ds(target, count)],
            send_sem=far_send.at[i],
            recv_sem=far_recv.at[i],
            device_id=rank_at(0, -1 if i % 2 else 1),
            device_id_type=MESH,
        )

    def late_copy(c, down, d):
        return pltpu.make_async_remote_copy(
            src_ref=late[c].at[down * xs + d],
            dst_ref=chosen[c].at[xs * early + (xs - d) % xs * 3 + down],
            send_sem=late_send.at[c, 0],
            recv_sem=late_recv.at[c],
            device_id=rank_at(d, -1 if down else 1),
            device_id_type=MESH,
        )

    def pass_copy(c, down):
        count = xs - few if down else few
        return pltpu.make_async_remote_copy(
            src_ref=late[c].at[pl.ds(2 * xs + down * few, count)],
            dst_ref=passed[c].at[pl.ds(down * few, count)],
            send_sem=pass_send.at[c, down],
            recv_sem=pass_recv.at[c, down],
            device_id=rank_at(0, -1 if down else 1),
            device_id_type=MESH,
        )

    def last_copy(c, d):
        return pltpu.make_async_remote_copy(
            src_ref=passed[c].at[d],
            dst_ref=chosen[c].at[xs * early + (xs - d) % xs * 3 + 2],
            send_sem=late_send.at[c, 1],
            recv_sem=late_recv.at[c],
            device_id=rank_at(d, 1 if d < few else -1),
            device_id_type=MESH,
        )

    def whole_late(c, source, i):
        return pltpu.make_async_remote_copy(
            src_ref=source,
            dst_ref=chosen[c].at[pl.ds(xs * early, source.shape[0])],
            send_sem=late_send.at[c, i],
            recv_sem=late_recv.at[c],
            device_id=rank_at(0, 1),
            device_id_type=MESH,
        )

    def pair_copy(c):
        return pltpu.make_async_remote_copy(
            src_ref=pair_out[c],
            dst_ref=pair_in[c],
            send_sem=pair_send.at[c],
            recv_sem=pair_recv.at[c],
            device_id={"grp": grp_at(0, 1)},
            device_id_type=MESH,
        )

    def sum_copy(c, dy):
        return pltpu.make_async_remote_copy(
            src_ref=outgoing[c].at[dy - 1],
            dst_ref=incoming[c].at[dy - 1],
            send_sem=sum_send.at[c],
            recv_sem=sum_recv.at[c],
            device_id={"grp": grp_at(dy)},
            device_id_type=MESH,
        )

    def whole_sum(c):
        return pltpu.make_async_remote_copy(
            src_ref=outgoing[c],
            dst_ref=incoming[c],
            send_sem=sum_send.at[c],
            recv_sem=sum_recv.at[c],
            device_id={"grp": grp_at(1)},
            device_id_type=MESH,
        )

    def make_tables():
        cols_copy.wait()
        lane = lax.broadcasted_iota(jnp.int32, (1, 128), 1)
        base = grp * (ranks * rows)

        def row(n, held):
            for k in range(width):
                local = cols[n, k] - base
                peer, within = lax.div(local, rows), lax.rem(local, rows)
                rx = lax.rem(lax.rem(peer, xs) - x + xs, xs)
                j = lax.rem(z - lax.div(peer, xs) + zs, zs)
                spot = jnp.where(j < half, 2 * j - 1, 2 * (zs - j))
                spot = jnp.where(j == half, zs - 1, jnp.maximum(spot, 0))
                spot = jnp.where(
                    spot < early,
                    rx * early + spot,
                    xs * early + rx * 3 + spot - early,
                )
                place[n * width + k] = jnp.where(peer == rank, ranks + within, spot)
                held = jnp.maximum(held, jnp.where(lane == peer, within, 0))
            return held

        table[0] = lax.fori_loop(0, rows, row, jnp.zeros((1, 128), jnp.int32))
        for d in range(1, xs):
            table_copy(d).start()

    def read_tables():
        for d in range(1, xs):
            table_copy(d).wait_recv()
        far_copy(0).start()
        far_copy(1).start()
        fetch_tables(0, xs)

    def fetch_tables(start, count):
        which = pl.ds(start, count)
        fetch = pltpu.make_async_copy(table.at[which], table_smem.at[which], table_sem)
        fetch.start()
        fetch.wait()

    def pass_tables():
        far_copy(0).wait_recv()
        far_copy(1).wait_recv()
        far_copy(2).start()
        far_copy(3).start()

    def read_far_tables():
        far_copy(2).wait_recv()
        far_copy(3).wait_recv()
        fetch_tables(xs, 3 * xs)

    def pick(blocks, index):
        held = blocks[0]
        for w in range(1, rows):
            held = jnp.where(index == w, blocks[w], held)
        return held

    def own(c):
        ring_copy(c, 1, 0).start()
        ring_copy(c, 1, 1).start()

    def send_late(c, down):
        j = half + 2 if down else full
        source = lax.rem(z - j + zs, zs) * xs + x
        blocks = [ring[c][early - full if down else full, w] for w in range(rows)]
        passing = range(few, xs) if down else range(few)
        for d in passing:
            late[c][2 * xs + d] = pick(blocks, table_smem[3 * xs + d, 0, source])
        pass_copy(c, down).start()
        for d in range(xs):
            index = table_smem[(1 if down else 2) * xs + d, 0, source]
            late[c][down * xs + d] = pick(blocks, index)
            late_copy(c, down, d).start()

    def step(c, s):
        if s == full + 1:
            for down in (0, 1):
                pass_copy(c, down).wait_recv()
                for d in range(few, xs) if down else range(few):
                    last_copy(c, d).start()
            return
        if s > 0:
            ring_copy(c, s, 0).wait_recv()
            ring_copy(c, s, 1).wait_recv()
        if s == full:
            send_late(c, 0)
            send_late(c, 1)
        elif s > 0:
            ring_copy(c, s + 1, 0).start()
            ring_copy(c, s + 1, 1).start()
        hops = [(0, 0)] if s == 0 else [(s, s), (zs - s, early - s)]
        start = 0 if s == 0 else 2 * s - 1
        for at, (j, held) in enumerate(hops):
            blocks = [ring[c][held, w] for w in range(rows)]
            spot = start + at
            source = lax.rem(z - j + zs, zs) * xs + x
            if j == 0:
                for w in range(rows):
                    chosen[c][ranks + w] = blocks[w]
                chosen[c][0] = blocks[0]
            else:
                chosen[c][spot] = pick(blocks, table_smem[0, 0, source])
            for d in range(1, xs):
                stage[c][d - 1, spot] = pick(blocks, table_smem[d, 0, source])
        for d in range(1, xs):
            x_copy(c, d, start, len(hops)).start()

    def turn(n):
        if n == 0:
            a_copy.wait()

        def block(e, carry):
            a_ref[e] = a_ref[e].T
            return carry

        lax.fori_loop(n * width, (n + 1) * width, block, 0, unroll=4)

    def multiply(c, piece):
        part = PARTS[c]
        if piece == 0:
            for d in range(1, xs):
                x_copy(c, d, 0, early).wait_recv()
            whole_late(c, late[c], 0).wait_recv()

        def row(n, carry):
            products = []
            for k in range(width):
                q = chosen[c][place[n * width + k]]
                product = jnp.dot(
                    q, a_ref[n * width + k], preferred_element_type=jnp.float32
                )
                products.append(product.astype(jnp.bfloat16))
            term = jnp.dot(
                jnp.concatenate(products, axis=0),
                p_ref[n],
                preferred_element_type=jnp.float32,
            )
            for s in range(SLOTS):
                held = jnp.zeros((part, order), jnp.float32)
                for k in range(width):
                    mine = term[k * part : (k + 1) * part]
                    held = held + jnp.where(slot[n, k] == s, mine, 0.0)
                sums[n, s, :part] = held
            return carry

        each = rows // PIECES
        lax.fori_loop(piece * each, (piece + 1) * each, row, 0, unroll=True)

    def gather_sums(c, dy, dc, s):
        part = PARTS[c]
        held = jnp.zeros((part, order), jnp.float32)
        for n in range(rows):
            mine = agg[n] == grp_at(dy, dc)
            held = held + jnp.where(mine, sums[n, s, :part], 0.0)
        return held

    def pair_sums(c):
        for dy in range(ys):
            for s in range(SLOTS):
                pair_out[c][dy, s] = gather_sums(c, dy, 1, s).astype(jnp.bfloat16)
        pair_copy(c).start()
        for dy in range(ys):
            for s in range(SLOTS):
                kept[c][dy, s] = gather_sums(c, dy, 0, s)

    def send_sums(c):
        pair_copy(c).wait_recv()
        for dy in sorted(range(1, ys), key=lambda dy: -min(dy, ys - dy)):
            for s in range(SLOTS):
                both = kept[c][dy, s] + pair_in[c][dy, s].astype(jnp.float32)
                outgoing[c][dy - 1, s] = both.astype(jnp.bfloat16)
            sum_copy(c, dy).start()

    def finish(c):
        mine = pl.ds(firsts[c], PARTS[c])
        for s in range(SLOTS):
            total[s, mine] = kept[c][0, s] + pair_in[c][0, s].astype(jnp.float32)
        whole_sum(c).wait_recv()
        for s in range(SLOTS):
            held = total[s, mine]
            for dy in range(1, ys):
                held = held + incoming[c][dy - 1, s].astype(jnp.float32)
            total[s, mine] = held

    pl.semaphore_wait(barrier, len(neighbours))
    work = []

    def put(hop, c, call, *args):
        key = hop + c * (LAG + LAG_GROWTH * min(max(hop, 0), half))
        work.append((key, len(work), call, (c, *args)))

    for c in range(chunks):
        put(-AHEAD, c, own)
        for s in range(half):
            put(s, c, step, s)
        key = half + READY
        for piece in range(PIECES):
            put(key + GAPS[0] * piece, c, multiply, piece)
        put(key + GAPS[0] + GAPS[1], c, pair_sums)
        put(key + sum(GAPS), c, send_sums)
    for n in range(rows):
        work.append((full * (0.2 + TURN * n), len(work), turn, (n,)))
    work.append((full * 0.4, len(work), pass_tables, ()))
    work.append((full * 0.9, len(work), read_far_tables, ()))
    work.sort(key=lambda task: task[:2])
    tabled = read = False
    for key, _, call, args in work:
        if call is step and not read:
            make_tables()
            read_tables()
            read = True
        if call is multiply and not tabled:
            for copy in (agg_copy, slot_copy):
                copy.wait()
            tabled = True
        call(*args)
    for c in range(chunks - 1):
        finish(c)
    for d in range(1, xs):
        table_copy(d).wait_send()
    for i in range(4):
        far_copy(i).wait_send()
    for c in range(chunks):
        for s in range(1, full + 1):
            ring_copy(c, s, 0).wait_send()
            ring_copy(c, s, 1).wait_send()
        for d in range(1, xs):
            x_copy(c, d, 0, early).wait_send()
        whole_late(c, late[c].at[pl.ds(0, 2 * xs)], 0).wait_send()
        whole_late(c, passed[c], 1).wait_send()
        for down in (0, 1):
            pass_copy(c, down).wait_send()
        pair_copy(c).wait_send()
        if c < chunks - 1:
            whole_sum(c).wait_send()
    finish(chunks - 1)
    for s in range(SLOTS):
        out_ref[0, s] = total[s].T.astype(jnp.bfloat16)
    whole_sum(chunks - 1).wait_send()


def on_device(xs, zs, a_blocks, a_cols, p_blocks, agg_grp, c_slot):
    rows, width, order = a_blocks.shape[:3]
    groups = lax.axis_size("grp")
    ys = groups // CORES
    ranks = lax.axis_size("rank")
    chunks = len(PARTS)
    full = zs // 2 - 2
    early = 2 * full + 1
    sizes = (xs, zs, groups, rows, width, order)
    dma = pltpu.SemaphoreType.DMA

    def parted(*shape, dtype=jnp.bfloat16):
        return [pltpu.VMEM((*shape, part, order), dtype) for part in PARTS]

    return pl.pallas_call(
        functools.partial(kernel, sizes),
        out_shape=pltpu.VMEM((1, SLOTS, order, order), jnp.bfloat16),
        in_specs=[pl.BlockSpec(memory_space=pltpu.HBM)] * 5,
        out_specs=pl.BlockSpec(memory_space=pltpu.VMEM),
        scratch_shapes=[
            pltpu.SMEM((rows, width), jnp.int32),
            pltpu.SMEM((rows,), jnp.int32),
            pltpu.SMEM((rows, width), jnp.int32),
            pltpu.VMEM((rows, order, order), jnp.bfloat16),
            pltpu.VMEM((rows * width, order, order), jnp.bfloat16),
            pltpu.VMEM((4 * xs, 1, 128), jnp.int32),
            pltpu.VMEM((rows, SLOTS, max(PARTS), order), jnp.float32),
            pltpu.VMEM((SLOTS, order, order), jnp.float32),
            pltpu.SMEM((4 * xs, 1, 128), jnp.int32),
            pltpu.SMEM((rows * width,), jnp.int32),
            dma((5,)),
            dma(()),
            dma((xs - 1,)),
            dma((xs - 1,)),
            dma((chunks, full, 2)),
            dma((chunks, full, 2)),
            dma((chunks, xs - 1)),
            dma((chunks, xs - 1)),
            dma((chunks,)),
            dma((chunks,)),
            dma((chunks,)),
            dma((chunks,)),
            dma((4,)),
            dma((4,)),
            dma((chunks, 2)),
            dma((chunks, 2)),
            dma((chunks, 2)),
            dma((chunks,)),
        ]
        + parted(early, rows)
        + parted(xs - 1, early)
        + parted(3 * xs)
        + parted(xs)
        + parted(ranks + rows)
        + parted(ys - 1, SLOTS)
        + parted(ys - 1, SLOTS)
        + parted(ys, SLOTS)
        + parted(ys, SLOTS)
        + parted(ys, SLOTS, dtype=jnp.float32),
        compiler_params=pltpu.CompilerParams(
            collective_id=0, has_side_effects=True, vmem_limit_bytes=62 << 20
        ),
        cost_estimate=pl.CostEstimate(
            flops=4 * rows * width * order**3,
            bytes_accessed=2 * rows * (width + 1) * order**2,
            transcendentals=0,
        ),
    )(a_cols, agg_grp, c_slot, p_blocks, a_blocks.reshape(rows * width, order, order))


def solution(mesh):
    in_specs = (
        P(("grp", "rank"), None, None, None),
        P(("grp", "rank"), None),
        P(("grp", "rank"), None, None),
        P(("grp", "rank")),
        P(("grp", "rank"), None),
    )
    out_specs = P(("grp", "rank"), None, None, None)
    return jax.shard_map(
        functools.partial(on_device, X, Z),
        mesh=mesh,
        in_specs=in_specs,
        out_specs=out_specs,
        check_vma=False,
    )
```
